32 devices in a mesh: ctx: 8 (over y, x, core), tp: 4 (over z).
Axes of the slice: x: 2, y: 2, z: 4, core: 2. Of those that a mesh axis runs over, the one named last changes fastest.
Arguments:
- queries: bfloat16 [16384, 8192], P('ctx', 'tp'), may hold values from -48 to 48
- keys: bfloat16 [16384, 1024], P(('ctx', 'tp')), may hold values from -6 to 6
- values: bfloat16 [16384, 1024], P(('ctx', 'tp')), may hold values from -6 to 6
- rope_factors: float32 [64], replicated, may hold values from 1 to 32
- doc_lengths: int32 [64], replicated, may hold values from 1 to 512, 16384 in all
- owner_map: int32 [8, 8], replicated, may hold values from 0 to 7, as said below
Outputs:
- attended: bfloat16 [16384, 8192], P('ctx', 'tp')
The draws below stay inside these ranges and needn't reach their ends.
Inputs may be any that keep to these rules, and one draw needn't show every extreme that they name: `owner_map`: row c lists the owners of the 8 blocks of index c: they are different devices, and every device owns exactly one block of each in-device number r, so exactly 8 blocks in all.
All inputs are finite; a program needn't handle non-finite values.
Results may differ from the reference program's by a relative error of at most 0.0051.
Values may be sent and summed in bfloat16 or wider, within the bound.
A program may use at most 128 MiB of HBM per device.

```python
import math
import jax
import jax.numpy as jnp
import numpy as np
from jax import lax

HEADS = 64
KV = 8
HD = 128
BLOCKS_DEV = 8
TOKENS = 16384
NDOCS = 64
MAXDOC = 512
N_CTX = 8


def key_field(key):
    base = jax.random.fold_in(key, 11)
    return jnp.clip(jax.random.normal(base, (TOKENS, KV * HD), jnp.float32), -6.0, 6.0)


def draw_keys(key, part):
    return key_field(key).astype(jnp.bfloat16)


def draw_queries(key, part):
    base = jax.random.fold_in(key, 23)
    return jnp.clip(jax.random.normal(base, (TOKENS, HEADS * HD), jnp.float32), -6.0, 6.0).astype(jnp.bfloat16)


def draw_owner_map(key, part):
    first_key = jax.random.fold_in(key, 41)
    second_key = jax.random.fold_in(key, 43)
    third_key = jax.random.fold_in(key, 47)
    first_perm = jax.random.permutation(first_key, N_CTX)
    second_perm = jax.random.permutation(second_key, N_CTX)
    offsets = jax.random.permutation(third_key, N_CTX)[:BLOCKS_DEV]
    lookup = (first_perm[:, None] + offsets[None, :]) % N_CTX
    return second_perm[lookup].astype(jnp.int32)


def shard_levels(stream_key, dims, pieces, smallest, largest):
    def one(axis_at, parts):
        heights = jax.random.uniform(jax.random.fold_in(jax.random.fold_in(stream_key, 6), axis_at), (parts,), jnp.float32, smallest / len(pieces), largest / len(pieces))
        return jnp.repeat(jnp.exp(heights), dims[axis_at] // parts).reshape((-1,) + (1,) * (len(dims) - axis_at - 1))

    level = one(*pieces[0])
    for cut in pieces[1:]:
        level = level * one(*cut)
    return level


def length_profile(number_of, total, bound, skew):
    portions = [(1 << 20) // math.isqrt(standing ** skew) + 1 for standing in range(2, number_of + 1)]
    spare, given = total - bound - (number_of - 1), [1] * (number_of - 1)
    while spare > 0:
        free = [i for i in range(number_of - 1) if given[i] < bound]
        whole, budget = sum([portions[i] for i in free]), spare
        for i in free:
            addition = min(bound - given[i], max(1, budget * portions[i] // whole), spare)
            given[i] = given[i] + addition
            spare = spare - addition
    return np.array([bound] + given)


def ragged_sizes(key, count, total, most, slope):
    if count == 2:
        one = jax.random.randint(key, (), max(1, total - most), min(most, total - 1) + 1)
        return jnp.stack([one, total - one])
    sizes = jnp.asarray(length_profile(count, total, most, slope), jnp.int32)
    pairs = (count - 1) // 2
    source_of, taker = sizes[1:1 + 2 * pairs:2], sizes[2:2 + 2 * pairs:2]
    room = jnp.minimum(source_of - 1, most - taker)
    shifted = jax.random.randint(jax.random.fold_in(key, 1), (pairs,), 0, 1 << 20) % (room + 1)
    sizes = sizes.at[1:1 + 2 * pairs:2].set(source_of - shifted).at[2:2 + 2 * pairs:2].set(taker + shifted)
    return sizes[jax.random.permutation(jax.random.fold_in(key, 2), count)]


def bell_draw(own_key, shape, spread, bound, pieces=(), kind=jnp.bfloat16):
    gain = shard_levels(own_key, shape, pieces, -0.22, 0.18) if pieces else 1.0
    entries = jax.random.normal(own_key, shape, jnp.float32) * spread * gain
    return jnp.minimum(jnp.maximum(entries, -bound), bound).astype(kind)


def setup_inputs(seed: int = 0) -> dict:
    streams_of = jax.random.split(jax.random.key(seed), 7)
    return {
        "queries": draw_queries(jax.random.fold_in(streams_of[6], 71), 0),
        "keys": draw_keys(jax.random.fold_in(streams_of[6], 71), 0),
        "values": bell_draw(streams_of[2], (TOKENS, KV * HD), 1.0, 6.0, ((0, 32),)),
        "rope_factors": jnp.clip(jnp.exp(jax.random.uniform(streams_of[3], (HD // 2,), jnp.float32, math.log(1.0), math.log(32.0))), 1.0, 32.0),
        "doc_lengths": ragged_sizes(streams_of[4], NDOCS, TOKENS, MAXDOC, 2).astype(jnp.int32),
        "owner_map": draw_owner_map(jax.random.fold_in(streams_of[6], 71), 0),
    }


THETA = 500000.0

def doc_tables(lengths, positions):
    doc_ends = jnp.cumsum(lengths, dtype=jnp.int32)
    before = positions[:, None] >= doc_ends[None, :]
    doc_index = lax.optimization_barrier(jnp.sum(before.astype(jnp.int32), axis=1, dtype=jnp.int32))
    doc_start = lax.optimization_barrier(jnp.sum(jnp.where(before, lengths[None, :], 0), axis=1, dtype=jnp.int32))
    return (doc_index, positions - doc_start)

def rotate(vectors, offsets, factors):
    half_dim = vectors.shape[-1] // 2
    exponent = jnp.arange(half_dim, dtype=jnp.float32) * (2.0 / vectors.shape[-1])
    inverse = 1.0 / (factors * jnp.power(jnp.float32(THETA), exponent))
    angles = offsets.astype(jnp.float32)[:, None] * inverse[None, :]
    cosine = jnp.cos(angles)[:, None, :]
    sine_part = jnp.sin(angles)[:, None, :]
    first_half = vectors[..., :half_dim]
    second_half = vectors[..., half_dim:]
    return jnp.concatenate([first_half * cosine - second_half * sine_part, second_half * cosine + first_half * sine_part], axis=-1)

def source_table(owner_map):
    ctx_size = owner_map.shape[0]
    devices = jnp.arange(ctx_size, dtype=jnp.int32)
    matches = owner_map[None, :, :] == devices[:, None, None]
    return lax.optimization_barrier(jnp.sum(jnp.where(matches, devices[None, :, None], 0), axis=1, dtype=jnp.int32))

def slot_rows(sources_row, per_dev, block_rows):
    blocks = sources_row * per_dev + jnp.arange(per_dev, dtype=jnp.int32)
    return (blocks[:, None] * block_rows + jnp.arange(block_rows, dtype=jnp.int32)[None, :]).reshape(-1)

def reference(queries, keys, values, rope_factors, doc_lengths, owner_map):
    total_rows = queries.shape[0]
    ctx_size = owner_map.shape[0]
    per_dev = owner_map.shape[1]
    row_count = total_rows // ctx_size
    block_rows = row_count // per_dev
    pad_rows = row_count // 4
    span = pad_rows + block_rows
    head_dim = 2 * rope_factors.shape[0]
    heads_all = queries.shape[1] // head_dim
    kv_all = keys.shape[1] // head_dim
    group_size = heads_all // kv_all
    score_scale = 1.0 / math.sqrt(head_dim)
    positions = jnp.arange(total_rows, dtype=jnp.int32)
    doc_index, offsets = doc_tables(doc_lengths, positions)
    q_rot = rotate(queries.astype(jnp.float32).reshape(total_rows, heads_all, head_dim), offsets, rope_factors).astype(jnp.bfloat16)
    k_rot = rotate(keys.astype(jnp.float32).reshape(total_rows, kv_all, head_dim), offsets, rope_factors).astype(jnp.bfloat16)
    v_all = values.reshape(total_rows, kv_all, head_dim)
    k_pad = jnp.concatenate([jnp.zeros((pad_rows, kv_all, head_dim), jnp.bfloat16), k_rot], axis=0)
    v_pad = jnp.concatenate([jnp.zeros((pad_rows, kv_all, head_dim), jnp.bfloat16), v_all], axis=0)
    pos_pad = jnp.arange(total_rows + pad_rows, dtype=jnp.int32) - pad_rows
    doc_pad = jnp.concatenate([jnp.full((pad_rows,), -1, jnp.int32), doc_index])

    def per_block(block_number):
        first = (block_number * block_rows).astype(jnp.int32)
        q_block = lax.dynamic_slice_in_dim(q_rot, first, block_rows).reshape(block_rows, kv_all, group_size, head_dim)
        k_block = lax.dynamic_slice_in_dim(k_pad, first, span)
        v_block = lax.dynamic_slice_in_dim(v_pad, first, span)
        pos_k = lax.dynamic_slice_in_dim(pos_pad, first, span)
        doc_k = lax.dynamic_slice_in_dim(doc_pad, first, span)
        pos_q = first + jnp.arange(block_rows, dtype=jnp.int32)
        doc_q = lax.dynamic_slice_in_dim(doc_index, first, block_rows)
        visible = (doc_q[:, None] == doc_k[None, :]) & (pos_k[None, :] <= pos_q[:, None]) & (pos_k[None, :] >= 0)
        scores = jnp.einsum('qkgd,jkd->kgqj', q_block.astype(jnp.float32), k_block.astype(jnp.float32)) * score_scale
        scores = jnp.where(visible[None, None], scores, -1e+30)
        row_peak = lax.optimization_barrier(jnp.max(scores, axis=-1, keepdims=True))
        weights = jnp.exp(scores - row_peak)
        row_total = lax.optimization_barrier(jnp.sum(weights, axis=-1, keepdims=True))
        mixture = jnp.einsum('kgqj,jkd->qkgd', weights.astype(jnp.bfloat16).astype(jnp.float32), v_block.astype(jnp.float32))
        result = (mixture / row_total.transpose(2, 0, 1, 3)).astype(jnp.bfloat16)
        return result.reshape(block_rows, heads_all * head_dim)
    gathered = lax.map(per_block, jnp.arange(total_rows // block_rows, dtype=jnp.int32))
    gathered = gathered.reshape(total_rows, heads_all * head_dim)
    sources = source_table(owner_map)

    def owner_slots(sources_row):
        return slot_rows(sources_row, per_dev, block_rows)
    slot_table = jax.vmap(owner_slots)(sources)
    return gathered[slot_table.reshape(-1)]
```

```python
import functools
import math

import jax
import jax.numpy as jnp
from jax import lax
from jax.experimental import pallas as pl
from jax.experimental.pallas import tpu as pltpu
from jax.sharding import PartitionSpec as P

THETA = 500000.0
BLOCK = 256
LANES = 128
MESH = pl.DeviceIdType.MESH


def flip(index, by, count):
    out, bit = 0, 1
    while bit < count:
        out = out + ((index // bit + by // bit) % 2) * bit
        bit *= 2
    return out


def turn(x, cosine, sine):
    return x * cosine + pltpu.roll(x, LANES // 2, 1) * sine


def fused_kernel(
    n, tp, kv_local, group, halo,
    lengths_ref, pick_ref, inv_ref, q_hbm, k_ref, v_hbm,
    land,
    qbuf, krot, kwins, vwins, cos_ref, sin_ref, start_ref, bias_ref, outbuf,
    kv_send, kv_recv, halo_send, halo_recv, out_send, out_recv, q_sem,
):
    c = lax.axis_index("ctx")
    t = lax.axis_index("tp")
    blocks = qbuf.shape[0]
    shard = k_ref.shape[0]
    rows = blocks * BLOCK
    span = halo + 1
    docs = lengths_ref.shape[0]
    after = (c + 1) % n

    barrier = pltpu.get_barrier_semaphore()
    for j in range(1, tp):
        pl.semaphore_signal(barrier, inc=1, device_id={"tp": (t + j) % tp}, device_id_type=MESH)
    for j in range(1, n):
        pl.semaphore_signal(barrier, inc=1, device_id={"ctx": (c + j) % n}, device_id_type=MESH)
    q_copy = pltpu.make_async_copy(q_hbm, qbuf, q_sem)
    q_copy.start()
    pl.semaphore_wait(barrier, tp + n - 2)

    def kv_copy(kind, g, j):
        peer = (t + j) % tp
        head = peer * kv_local + g
        if kind == 0:
            src, dst = krot.at[head], kwins[g]
        else:
            column = pl.multiple_of(head * LANES, LANES)
            src, dst = v_hbm.at[:, :, pl.ds(column, LANES)], vwins[g]
        dst = dst.at[pl.ds(halo + t * shard, shard)]
        if j == 0:
            return pltpu.make_async_copy(src, dst, kv_recv.at[kind, g, 0])
        return pltpu.make_async_remote_copy(
            src_ref=src, dst_ref=dst, send_sem=kv_send.at[kind, g, j],
            recv_sem=kv_recv.at[kind, g, j], device_id={"tp": peer}, device_id_type=MESH,
        )

    def halo_copy(kind, g):
        win = (kwins, vwins)[kind][g]
        return pltpu.make_async_remote_copy(
            src_ref=win.at[pl.ds(blocks, halo)], dst_ref=win.at[pl.ds(0, halo)],
            send_sem=halo_send.at[kind, g], recv_sem=halo_recv.at[kind, g],
            device_id={"ctx": after}, device_id_type=MESH,
        )

    def send_kv(kind, g):
        for j in range(tp):
            kv_copy(kind, g, j).start()

    def pass_halo(g):
        for kind in (1, 0):
            kv_copy(kind, g, 0).wait()
            for j in range(1, tp):
                kv_copy(kind, g, j).wait_recv()
        for kind in (1, 0):
            halo_copy(kind, g).start()

    send_kv(1, 0)

    lane = lax.broadcasted_iota(jnp.int32, (BLOCK, LANES), 1)
    line = lax.broadcasted_iota(jnp.int32, (BLOCK, LANES), 0)

    def tables(i, carry):
        b = (t * shard + i) % blocks
        at = c * rows + b * BLOCK + line

        def one(d, state):
            end, start = state
            end = end + lengths_ref[d]
            return end, jnp.where(at >= end, end, start)

        end, start = lax.fori_loop(0, docs, one, (jnp.int32(0), jnp.zeros_like(at)))
        angle = (at - start).astype(jnp.float32) * inv_ref[...]
        sine = jnp.sin(angle)
        cos_ref[b] = jnp.cos(angle)
        sin_ref[b] = jnp.where(lane < LANES // 2, -sine, sine)
        start_ref[b] = start - c * rows
        return carry

    lax.fori_loop(0, shard, tables, 0)

    def turn_keys(i, carry):
        b = t * shard + i
        for head in range(tp * kv_local):
            x = k_ref[i, :, head * LANES:(head + 1) * LANES].astype(jnp.float32)
            krot[head, i] = turn(x, cos_ref[b], sin_ref[b]).astype(jnp.bfloat16)
        return carry

    lax.fori_loop(0, shard, turn_keys, 0)
    send_kv(0, 0)
    for g in range(1, kv_local):
        send_kv(1, g)
        send_kv(0, g)
    lax.fori_loop(shard, blocks, tables, 0)

    q_copy.wait()
    step_rows = BLOCK // 4

    def turn_queries(i, carry):
        b = i // 4
        part = pl.ds(pl.multiple_of((i % 4) * step_rows, step_rows), step_rows)
        cosine, sine = cos_ref[b, part, :], sin_ref[b, part, :]
        for head in range(kv_local * group):
            cols = slice(head * LANES, (head + 1) * LANES)
            x = qbuf[b, part, cols].astype(jnp.float32)
            qbuf[b, part, cols] = turn(x, cosine, sine).astype(jnp.bfloat16)
        return carry

    lax.fori_loop(0, blocks * 4, turn_queries, 0)

    factor = math.log2(math.e) / math.sqrt(LANES)
    pairs = n // 2 - 1

    def out_copy(g, s):
        if isinstance(s, int) and s == 0:
            return pltpu.make_async_copy(outbuf.at[g, 0], land.at[g, 0], out_recv.at[g, 0])
        return pltpu.make_async_remote_copy(
            src_ref=outbuf.at[g, s], dst_ref=land.at[g, s], send_sem=out_send.at[g, s],
            recv_sem=out_recv.at[g, s], device_id={"ctx": flip(c, s, n)}, device_id_type=MESH,
        )

    pass_halo(0)
    for g in range(kv_local):
        for kind in (1, 0):
            halo_copy(kind, g).wait_recv()

        def step(i, carry, g=g):
            far = 2 * (i % pairs + 1) + i // pairs
            s = jnp.where(i < 2 * pairs, far, n - 1 - i)
            r = pick_ref[s]
            start = start_ref[r]
            own = r * BLOCK + line
            for tile in range(span * BLOCK // LANES):
                at = (r - halo) * BLOCK + tile * LANES + lane
                seen = (at >= start) & (at <= own)
                bias_ref[:, tile * LANES:(tile + 1) * LANES] = jnp.where(seen, 0.0, -1e30)
            k_win = kwins[g][pl.ds(r, span)].reshape(span * BLOCK, LANES)
            v_win = vwins[g][pl.ds(r, span)].reshape(span * BLOCK, LANES)
            for h in range(group):
                q = qbuf[r, :, (g * group + h) * LANES:(g * group + h + 1) * LANES]
                scores = lax.dot_general(
                    q, k_win, (((1,), (1,)), ((), ())), preferred_element_type=jnp.float32
                ) + bias_ref[...]
                peak = jnp.max(scores, axis=1, keepdims=True)
                weight = jnp.exp2((scores - peak) * factor)
                total = jnp.sum(weight, axis=1, keepdims=True)
                mixed = jnp.dot(
                    weight.astype(jnp.bfloat16), v_win, preferred_element_type=jnp.float32
                )
                outbuf[g, s, :, h * LANES:(h + 1) * LANES] = (mixed * (1.0 / total)).astype(
                    jnp.bfloat16
                )

            @pl.when(i < n - 1)
            def _():
                out_copy(g, s).start()

            if g + 1 < kv_local:
                @pl.when(i == n // 2)
                def _():
                    pass_halo(g + 1)

            return carry

        lax.fori_loop(0, n, step, 0)
        out_copy(g, 0).start()

    for g in range(kv_local):
        for kind in (1, 0):
            for j in range(1, tp):
                kv_copy(kind, g, j).wait_send()
            halo_copy(kind, g).wait_send()
        out_copy(g, 0).wait()

        def finish(s, carry, g=g):
            out_copy(g, s).wait()
            return carry

        lax.fori_loop(1, n, finish, 0)


def place_kernel(where_ref, land_ref, out_ref):
    out_ref[...] = land_ref[0, 0]


def local(n, tp, queries, keys, values, rope_factors, doc_lengths, owner_map):
    c = lax.axis_index("ctx")
    rows, q_width = queries.shape
    blocks = owner_map.shape[1]
    head_dim = 2 * rope_factors.shape[0]
    kv_heads = keys.shape[1] // head_dim
    kv_local = kv_heads // tp
    group = q_width // head_dim // kv_local
    shard = keys.shape[0] // BLOCK
    halo = rows // 4 // BLOCK
    width = group * head_dim

    exponent = jnp.arange(head_dim // 2, dtype=jnp.float32) * (2.0 / head_dim)
    inverse = 1.0 / (rope_factors * jnp.power(jnp.float32(THETA), exponent))
    inverse = jnp.concatenate([inverse, inverse])[None, :]
    steps = jnp.arange(n, dtype=jnp.int32)
    partner = c ^ steps
    mine = lax.dynamic_index_in_dim(owner_map, c, 0, keepdims=False)
    slots = jnp.arange(blocks, dtype=jnp.int32)
    pick = jnp.sum(jnp.where(mine[None, :] == partner[:, None], slots[None, :], 0), axis=1)
    source = jnp.sum(jnp.where(owner_map == c, steps[:, None], 0), axis=0)
    where = c ^ source

    vmem = pl.BlockSpec(memory_space=pltpu.VMEM)
    smem = pl.BlockSpec(memory_space=pltpu.SMEM)
    anywhere = pl.BlockSpec(memory_space=pl.ANY)
    window = pltpu.VMEM((halo + blocks, BLOCK, LANES), jnp.bfloat16)
    table = pltpu.VMEM((blocks, BLOCK, LANES), jnp.float32)
    dma = pltpu.SemaphoreType.DMA
    landed = pl.pallas_call(
        functools.partial(fused_kernel, n, tp, kv_local, group, halo),
        out_shape=jax.ShapeDtypeStruct((kv_local, n, BLOCK, width), jnp.bfloat16),
        in_specs=[smem, smem, vmem, anywhere, vmem, anywhere],
        out_specs=anywhere,
        scratch_shapes=[
            pltpu.VMEM((blocks, BLOCK, q_width), jnp.bfloat16),
            pltpu.VMEM((kv_heads, shard, BLOCK, LANES), jnp.bfloat16),
            [window] * kv_local,
            [window] * kv_local,
            table,
            table,
            pltpu.VMEM((blocks, BLOCK, LANES), jnp.int32),
            pltpu.VMEM((BLOCK, (halo + 1) * BLOCK), jnp.float32),
            pltpu.VMEM((kv_local, n, BLOCK, width), jnp.bfloat16),
            dma((2, kv_local, tp)),
            dma((2, kv_local, tp)),
            dma((2, kv_local)),
            dma((2, kv_local)),
            dma((kv_local, n)),
            dma((kv_local, n)),
            dma,
        ],
        compiler_params=pltpu.CompilerParams(
            collective_id=0, has_side_effects=True, vmem_limit_bytes=52 * 2**20
        ),
        name="attend_and_send",
    )(
        doc_lengths,
        pick.astype(jnp.int32),
        inverse,
        queries.reshape(blocks, BLOCK, q_width),
        keys.reshape(shard, BLOCK, kv_heads * head_dim),
        values.reshape(shard, BLOCK, kv_heads * head_dim),
    )
    return pl.pallas_call(
        place_kernel,
        grid_spec=pltpu.PrefetchScalarGridSpec(
            num_scalar_prefetch=1,
            grid=(blocks, kv_local),
            in_specs=[
                pl.BlockSpec((1, 1, BLOCK, width), lambda b, g, where: (g, where[b], 0, 0))
            ],
            out_specs=pl.BlockSpec((BLOCK, width), lambda b, g, where: (b, g)),
        ),
        out_shape=jax.ShapeDtypeStruct((rows, q_width), jnp.bfloat16),
        name="place_blocks",
    )(where.astype(jnp.int32), landed)


def solution(mesh):
    n, tp = mesh.shape["ctx"], mesh.shape["tp"]
    in_specs = (P("ctx", "tp"), P(("ctx", "tp"), None), P(("ctx", "tp"), None), P(), P(), P())
    return jax.shard_map(
        functools.partial(local, n, tp),
        mesh=mesh, in_specs=in_specs, out_specs=P("ctx", "tp"), check_vma=False,
    )
```
